32 devices in a mesh: groups: 2 (over y), tm: 8 (over z, x), space: 2 (over core).
Axes of the slice: x: 2, y: 2, z: 4, core: 2. Of those that a mesh axis runs over, the one named last changes fastest.
Arguments:
- iterate: float32 [16, 64, 512], P(('groups', 'tm'), None, 'space'), parts along dimension 0, may hold values from -6 to 6
- forcing: bfloat16 [64, 64, 512], P(('groups', 'tm'), None, 'space'), parts along dimension 0, may hold values from -6 to 6
- initial: float32 [128, 512], P('groups', 'space'), parts along dimension 0, may hold values from -6 to 6
- self_block: float32 [64, 64], replicated, may hold values from -0.5 to 1
- face_blocks: float32 [6, 64, 64], replicated, may hold values from -0.075 to 0.075
- element_gain: float32 [512], P('space'), may hold values from 0.5 to 1.5
- neighbors: int32 [6, 512], P(None, 'space'), may hold values from 0 to 319, as said below
- face_mask: int32 [6, 512], P(None, 'space'), may hold values from 0 to 1
- coarse_decay: bfloat16 [16, 64, 512], P(('groups', 'tm'), None, 'space'), parts along dimension 0, may hold values from 0 to 1
Outputs:
- fine_states: float32 [64, 64, 512], P(('groups', 'tm'), None, 'space'), parts along dimension 0
The draws below stay inside these ranges and needn't reach their ends.
There are 2 independent parts, one for each index of `groups`. The reference program is written for one: setup_inputs(seed, part) draws one part's arguments, and reference() takes and returns one part's arrays. A program takes and returns all parts, laid end to end along the dimension named above; an argument that names none is the same for every part. Nothing has to cross between parts.
Inputs may be any that keep to these rules, and one draw needn't show every extreme that they name: `neighbors`: for element j of space block s, a value v < 256 names element s * 256 + v of the same block; a value v >= 256 names element (1 - s) * 256 + v - 64 of the other block, which is one of that block's last 64 elements; where face_mask is 0 the value is 0.
All inputs are finite; a program needn't handle non-finite values.
Results may differ from the reference program's by a relative error of at most 0.0003.
Values sent between devices are 32-bit elements; how exact they have to be, the bound alone decides.
A program may use at most 64 MiB of HBM per device.

```python
import math
import jax
import jax.numpy as jnp
from jax import lax

DOFS = 64
CF = 4
GX = 8
GY = 4
GZ = 8
E_DEV = 256
BND = 64
E_TOT = 512
CRUDE_PERIODS = 8
N_T = 32


def grid_tables(key):
    plane = GY * GZ
    orders = []
    slots = []
    for block_id in range(2):
        subkey = jax.random.fold_in(key, 101 + block_id)
        key_inner, key_lower, key_upper = jax.random.split(subkey, 3)
        interior = jax.random.permutation(key_inner, jnp.arange(plane, E_DEV - plane, dtype=jnp.int32))
        lower = jax.random.permutation(key_lower, jnp.arange(0, plane, dtype=jnp.int32))
        upper = jax.random.permutation(key_upper, jnp.arange(E_DEV - plane, E_DEV, dtype=jnp.int32))
        order = jnp.concatenate([interior, lower, upper]).astype(jnp.int32)
        orders.append(order)
        slots.append(jnp.argsort(order).astype(jnp.int32))
    tables = []
    masks = []
    for block_id in range(2):
        grid_id = orders[block_id]
        own = slots[block_id]
        far = slots[1 - block_id]
        xpos = grid_id // plane
        ypos = grid_id // GZ % GY
        zpos = grid_id % GZ
        across = ypos * GZ + zpos
        plus_x = jnp.where(xpos + 1 < GX, own[jnp.minimum(grid_id + plane, E_DEV - 1)], far[across] + BND)
        minus_x = jnp.where(xpos > 0, own[jnp.maximum(grid_id - plane, 0)], far[(GX - 1) * plane + across] + BND)
        has_py = ypos + 1 < GY
        has_my = ypos > 0
        has_pz = zpos + 1 < GZ
        has_mz = zpos > 0
        plus_y = jnp.where(has_py, own[jnp.minimum(grid_id + GZ, E_DEV - 1)], 0)
        minus_y = jnp.where(has_my, own[jnp.maximum(grid_id - GZ, 0)], 0)
        plus_z = jnp.where(has_pz, own[jnp.minimum(grid_id + 1, E_DEV - 1)], 0)
        minus_z = jnp.where(has_mz, own[jnp.maximum(grid_id - 1, 0)], 0)
        tables.append(jnp.stack([plus_x, minus_x, plus_y, minus_y, plus_z, minus_z]).astype(jnp.int32))
        always = jnp.ones_like(grid_id)
        masks.append(jnp.stack([always, always, has_py.astype(jnp.int32), has_my.astype(jnp.int32), has_pz.astype(jnp.int32), has_mz.astype(jnp.int32)]).astype(jnp.int32))
    return (jnp.concatenate(tables, axis=1), jnp.concatenate(masks, axis=1))


def draw_neighbors(key, part):
    index_table, mask_table = grid_tables(key)
    return index_table


def draw_face_mask(key, part):
    index_table, mask_table = grid_tables(key)
    return mask_table


def draw_self_block(key, part):
    key = jax.random.fold_in(key, 7)
    noise = jax.random.normal(key, (DOFS, DOFS), jnp.float32)
    return 0.5 * jnp.eye(DOFS, dtype=jnp.float32) + 0.3 * noise / math.sqrt(DOFS)


def draw_coarse_decay(key, part):
    key = jax.random.fold_in(key, 11)
    stochastic_seeds = jax.random.split(key, 6)
    slow_share = 0.5
    slow = jax.random.uniform(stochastic_seeds[0], (1, DOFS, E_TOT)) < slow_share
    slow_rate = jax.random.uniform(stochastic_seeds[1], (1, DOFS, E_TOT), jnp.float32, 0.05, 0.6) / CRUDE_PERIODS
    fast_rate = jax.random.uniform(stochastic_seeds[2], (1, DOFS, E_TOT), jnp.float32, 0.5, 2.5)
    damping_speed = jnp.where(slow, slow_rate, fast_rate)
    stride_scaling = jnp.exp(jax.random.uniform(stochastic_seeds[3], (CRUDE_PERIODS, 1, 1), jnp.float32, 0.0, math.log(2.0)))
    spike_height = jax.random.uniform(stochastic_seeds[4], (CRUDE_PERIODS, 1, 1)) < 3.0 / CRUDE_PERIODS
    clipping_limit = jax.random.uniform(stochastic_seeds[5], (CRUDE_PERIODS, DOFS, E_TOT), jnp.float32, 0.5, 0.8)
    damping_ratio = jnp.exp(-damping_speed * stride_scaling) * jnp.where(spike_height, clipping_limit, 1.0)
    return damping_ratio.astype(jnp.bfloat16)


def block_levels(rng, extent, cuts, least, top_value):
    def one(dim, shards_of):
        steps = jax.random.uniform(jax.random.fold_in(jax.random.fold_in(rng, 6), dim), (shards_of,), jnp.float32, least / len(cuts), top_value / len(cuts))
        return jnp.repeat(jnp.exp(steps), extent[dim] // shards_of).reshape((-1,) + (1,) * (len(extent) - dim - 1))

    loudness = one(*cuts[0])
    for cut in cuts[1:]:
        loudness = loudness * one(*cut)
    return loudness


def normal_values(key, extent, spread, limit, shards=(), held_as=jnp.bfloat16):
    array = spread * jax.random.normal(key, extent, jnp.float32)
    if shards:
        array = array * block_levels(key, extent, shards, -0.22, 0.18)
    return jnp.clip(array, -limit, limit).astype(held_as)


def setup_inputs(seed: int = 0, part: int = 0) -> dict:
    streams_of = jax.random.split(jax.random.key(seed), 10)
    part_keys = jax.random.split(jax.random.fold_in(streams_of[9], part), 10)
    return {
        "iterate": normal_values(part_keys[0], (CRUDE_PERIODS, DOFS, E_TOT), 1.0, 6.0, ((0, 8), (2, 2)), jnp.float32),
        "forcing": normal_values(part_keys[1], (N_T, DOFS, E_TOT), 1.0, 6.0, ((0, 8), (2, 2))),
        "initial": normal_values(part_keys[2], (DOFS, E_TOT), 1.0, 6.0, ((1, 2),), jnp.float32),
        "self_block": draw_self_block(jax.random.fold_in(streams_of[9], 71), part),
        "face_blocks": normal_values(streams_of[4], (6, DOFS, DOFS), 0.0125, 0.075, (), jnp.float32),
        "element_gain": jnp.clip(jnp.exp(math.log(1.5) - 1.0986123 * jax.random.uniform(streams_of[5], (E_TOT,), jnp.float32) ** block_levels(streams_of[5], (E_TOT,), ((0, 2),), -0.2, 0.2)), 0.5, 1.5),
        "neighbors": draw_neighbors(jax.random.fold_in(streams_of[9], 71), part),
        "face_mask": draw_face_mask(jax.random.fold_in(streams_of[9], 71), part),
        "coarse_decay": draw_coarse_decay(jax.random.fold_in(jax.random.fold_in(streams_of[9], part), 71), part),
    }


highest = lax.Precision.HIGHEST


def global_index(neighbors):
    column = jnp.arange(E_TOT, dtype=jnp.int32)
    block_id = column // E_DEV
    inside = block_id * E_DEV + neighbors
    across = (1 - block_id) * E_DEV + neighbors - BND
    return jnp.where(neighbors < E_DEV, inside, across).astype(jnp.int32)


def propagate(state_field, self_block, face_blocks, element_gain, lookup, weights):
    summed = jnp.einsum("ij,kje->kie", self_block, state_field, precision=highest)
    for face_id in range(6):
        nearby = jnp.take(state_field, lookup[face_id], axis=2) * weights[face_id]
        summed = summed + jnp.einsum("ij,kje->kie", face_blocks[face_id], nearby, precision=highest)
    return summed * element_gain


def reference(iterate, forcing, initial, self_block, face_blocks, element_gain, neighbors, face_mask, coarse_decay):
    lookup = global_index(neighbors)
    weights = face_mask.astype(jnp.float32)
    sources = forcing.astype(jnp.float32).reshape(CRUDE_PERIODS, CF, DOFS, E_TOT)
    incoming_c = jnp.concatenate([initial[None], iterate[:-1]], axis=0)
    current = incoming_c
    for section in range(CF):
        current = propagate(current, self_block, face_blocks, element_gain, lookup, weights) + sources[:, section]
    residual = current - iterate
    damping_ratio = coarse_decay.astype(jnp.float32)

    def advance(carried, inputs):
        damping_speed, term = inputs
        return damping_speed * carried + term, carried

    _, incoming = lax.scan(advance, jnp.zeros((DOFS, E_TOT), jnp.float32), (damping_ratio, residual))
    corrected = iterate + (damping_ratio * incoming + residual)
    current = incoming_c + incoming
    outputs = []
    for section in range(CF - 1):
        current = propagate(current, self_block, face_blocks, element_gain, lookup, weights) + sources[:, section]
        outputs.append(current)
    outputs.append(corrected)
    return jnp.stack(outputs, axis=1).reshape(N_T, DOFS, E_TOT)
```

```python
import functools

import jax
import jax.numpy as jnp
from jax import lax
from jax.experimental import pallas as pl
from jax.experimental.pallas import tpu as pltpu
from jax.sharding import PartitionSpec as P

CF = 4
BND = 64
LANES = 128
MESH = pl.DeviceIdType.MESH


def radices(count):
    out = []
    while count > 1:
        for m in (4, 2, count):
            if count % m == 0:
                out.append(m)
                count //= m
                break
    return out or [1]


def kernel(
    count,
    stages,
    iterate,
    forcing,
    initial,
    self_block,
    face_blocks,
    gain,
    neighbors,
    face_mask,
    decay,
    out,
    start,
    cur,
    source,
    partner_source,
    where_from,
    gains,
    weights,
    high,
    low,
    residual,
    entering,
    rslots,
    dslots,
    core_send,
    core_recv,
    step_send,
    step_recv,
    rsend,
    rrecv,
    dsend,
    drecv,
):
    f32, bf16 = jnp.float32, jnp.bfloat16
    g, t, s = (lax.axis_index(a) for a in ("groups", "tm", "space"))
    other = (g, t, 1 - s)
    rows, width = initial.shape

    digits, strides, stride = [], [], 1
    for m in stages:
        digits.append(lax.rem(t // stride, m))
        strides.append(stride)
        stride *= m

    barrier = pltpu.get_barrier_semaphore()
    pl.semaphore_signal(barrier, inc=1, device_id=other, device_id_type=MESH)
    greeted = 1
    if count > 1:
        for by in (1, count - 1):
            for core in (s, 1 - s):
                there = (g, lax.rem(t + by, count), core)
                pl.semaphore_signal(barrier, inc=1, device_id=there, device_id_type=MESH)
                greeted += 1
        for m, digit, stride in zip(stages, digits, strides):
            for by in range(1, m):
                to = t + (lax.rem(digit + by, m) - digit) * stride
                pl.semaphore_signal(barrier, inc=1, device_id=(g, to, s), device_id_type=MESH)
                greeted += 1

    tables = neighbors[...]
    where_from[0, 0:6, :] = jnp.where(face_mask[...] == 0, -1, tables)
    where_from[0, 6:8, :] = jnp.zeros((2, width), jnp.int32)
    gains[0] = jnp.broadcast_to(gain[...][None, :], (8, width))
    source[...] = forcing[...].astype(f32)
    pl.semaphore_wait(barrier, greeted)

    def to_core(src, dst, i):
        return pltpu.make_async_remote_copy(
            src, dst, core_send.at[i], core_recv.at[i], device_id=other, device_id_type=MESH
        )

    def shift(i):
        core = s if i == 0 else 1 - s
        to = lax.rem(t + 1, count)
        return pltpu.make_async_remote_copy(
            iterate.at[0],
            start.at[i],
            step_send.at[i],
            step_recv.at[i],
            device_id=(g, to, core),
            device_id_type=MESH,
        )

    first_half = to_core(initial, start.at[1], 0)
    table_copy = to_core(where_from.at[0], where_from.at[1], 1)
    gain_copy = to_core(gains.at[0], gains.at[1], 2)
    source_copy = to_core(source.at[pl.ds(0, CF - 1)], partner_source, 3)
    entering_copy = to_core(entering.at[0], entering.at[1], 4)

    if count > 1:

        @pl.when(t < count - 1)
        def _():
            shift(0).start()
            shift(1).start()

    @pl.when(t == 0)
    def _():
        first_half.start()

    table_copy.start()
    gain_copy.start()
    source_copy.start()

    def link(slots, send, recv, i, b):
        digit = digits[i]
        base = sum(stages[:i])
        return pltpu.make_async_remote_copy(
            slots.at[base + digit],
            slots.at[base + digit],
            send.at[base + b],
            recv.at[base + digit],
            device_id=(g, t + (b - digit) * strides[i], s),
            device_id_type=MESH,
        )

    def arrival(slots, send, recv, i, b):
        base = sum(stages[:i])
        return pltpu.make_async_remote_copy(
            slots.at[base + b],
            slots.at[base + b],
            send.at[base + b],
            recv.at[base + b],
            device_id=(g, t, s),
            device_id_type=MESH,
        )

    def each_out(i, act):
        for b in range(stages[i]):
            last = i == len(stages) - 1
            pl.when(b > digits[i] if last else b != digits[i])(functools.partial(act, b))

    def each_in(i, act):
        for b in range(stages[i]):
            last = i == len(stages) - 1
            pl.when(b < digits[i] if last else b != digits[i])(functools.partial(act, b))

    def send(slots, ss, rs, i, value):
        slots[sum(stages[:i]) + digits[i]] = value
        each_out(i, lambda b: link(slots, ss, rs, i, b).start())

    def receive(slots, ss, rs, i):
        each_in(i, lambda b: arrival(slots, ss, rs, i, b).wait_recv())

    damping = decay[0].astype(f32)
    send(dslots, dsend, drecv, 0, damping)

    blocks = jnp.concatenate([self_block[...]] + [face_blocks[f] for f in range(6)], axis=1)
    upper = blocks.astype(bf16)
    weights[0:rows, :] = upper
    weights[rows : 2 * rows, :] = (blocks - upper.astype(f32)).astype(bf16)

    def put(r, cols, value):
        top = value.astype(bf16)
        high[r * rows : (r + 1) * rows, cols] = top
        low[r * rows : (r + 1) * rows, cols] = (value - top.astype(f32)).astype(bf16)

    def advance(field, halves):
        for h in range(halves):
            near = [field[h, :, LANES * i : LANES * (i + 1)] for i in range(width // LANES)]
            far = field[1 - h, :, width - LANES :]
            for i in range(width // LANES):
                cols = slice(h * width + LANES * i, h * width + LANES * (i + 1))
                put(0, cols, near[i])
                for f in range(6):
                    v = where_from[h, f : f + 1, LANES * i : LANES * (i + 1)]
                    lane = lax.bitwise_and(jnp.where(v >= width, v - BND, v), LANES - 1)
                    lane = jnp.broadcast_to(lane, (rows, LANES))
                    v = jnp.broadcast_to(v, (rows, LANES))
                    got = jnp.take_along_axis(far, lane, axis=1)
                    for k in reversed(range(width // LANES)):
                        here = jnp.take_along_axis(near[k], lane, axis=1)
                        got = jnp.where(v < LANES * (k + 1), here, got)
                    put(f + 1, cols, jnp.where(v < 0, 0.0, got))
        n = halves * width
        both = jnp.dot(weights[...], high[:, :n], preferred_element_type=f32)
        rest = jnp.dot(weights[0:rows, :], low[:, :n], preferred_element_type=f32)
        total = both[:rows] + (both[rows:] + rest)
        return [total[:, h * width : (h + 1) * width] * gains[h, 0:1, :] for h in range(halves)]

    if count > 1:

        @pl.when(t > 0)
        def _():
            shift(0).wait_recv()
            shift(1).wait_recv()

    @pl.when(t == 0)
    def _():
        start[0] = initial[...]
        first_half.wait_recv()

    table_copy.wait_recv()
    gain_copy.wait_recv()

    def decay_stage(i, product, before):
        receive(dslots, dsend, drecv, i)
        base = sum(stages[:i])
        lead = jnp.ones((rows, width), f32)
        whole = lead
        for b in range(stages[i]):
            part = dslots[base + b]
            lead = jnp.where(b < digits[i], lead * part, lead)
            whole = whole * part
        return whole, before * lead

    befores = [jnp.ones((rows, width), f32)]
    product = damping
    field = start
    for j in range(CF):
        got = advance(field, 2 if j < CF - 1 else 1)
        if j == 0:
            source_copy.wait_recv()
        if j < CF - 1:
            cur[0] = got[0] + source[j]
            cur[1] = got[1] + partner_source[j]
            field = cur
        if j == 1:
            for i in range(len(stages) - 1):
                product, after = decay_stage(i, product, befores[-1])
                befores.append(after)
                send(dslots, dsend, drecv, i + 1, product)
    local = (got[0] + source[CF - 1]) - iterate[0]
    residual[...] = local

    term = local
    prefix = jnp.zeros((rows, width), f32)
    for i in range(len(stages)):
        send(rslots, rsend, rrecv, i, term)
        base = sum(stages[:i])
        if i == len(stages) - 1:
            receive(dslots, dsend, drecv, i)
        receive(rslots, rsend, rrecv, i)
        carried = jnp.zeros((rows, width), f32)
        whole = carried
        for b in range(stages[i]):
            r, d = rslots[base + b], dslots[base + b]
            carried = jnp.where(b < digits[i], d * carried + r, carried)
            if i < len(stages) - 1:
                whole = d * whole + r
        prefix = prefix + befores[i] * carried
        term = whole
    entering[0] = prefix
    entering_copy.start()
    cur[0] = start[0] + prefix
    out[CF - 1] = iterate[0] + (damping * prefix + residual[...])
    entering_copy.wait_recv()
    cur[1] = start[1] + entering[1]
    for j in range(CF - 1):
        got = advance(cur, 2 if j < CF - 2 else 1)
        out[j] = got[0] + source[j]
        if j < CF - 2:
            cur[0] = out[j]
            cur[1] = got[1] + partner_source[j]

    for copy in (table_copy, gain_copy, source_copy, entering_copy):
        copy.wait_send()

    @pl.when(t == 0)
    def _():
        first_half.wait_send()

    if count > 1:

        @pl.when(t < count - 1)
        def _():
            shift(0).wait_send()
            shift(1).wait_send()

    for i in range(len(stages)):
        each_out(i, lambda b: link(dslots, dsend, drecv, i, b).wait_send())
        each_out(i, lambda b: link(rslots, rsend, rrecv, i, b).wait_send())


def solution(mesh):
    count = mesh.shape["tm"]
    stages = radices(count)
    slots = sum(stages)

    def local(iterate, forcing, initial, *rest):
        rows, width = initial.shape
        f32 = jnp.float32
        vmem = pl.BlockSpec(memory_space=pltpu.VMEM)
        dma = pltpu.SemaphoreType.DMA
        field = (rows, width)
        return pl.pallas_call(
            functools.partial(kernel, count, stages),
            out_shape=jax.ShapeDtypeStruct((CF, rows, width), f32),
            in_specs=[vmem] * 9,
            out_specs=vmem,
            scratch_shapes=[
                pltpu.VMEM((2,) + field, f32),
                pltpu.VMEM((2,) + field, f32),
                pltpu.VMEM((CF,) + field, f32),
                pltpu.VMEM((CF - 1,) + field, f32),
                pltpu.VMEM((2, 8, width), jnp.int32),
                pltpu.VMEM((2, 8, width), f32),
                pltpu.VMEM((2 * rows, 7 * rows), jnp.bfloat16),
                pltpu.VMEM((7 * rows, 2 * width), jnp.bfloat16),
                pltpu.VMEM((7 * rows, 2 * width), jnp.bfloat16),
                pltpu.VMEM(field, f32),
                pltpu.VMEM((2,) + field, f32),
                pltpu.VMEM((slots,) + field, f32),
                pltpu.VMEM((slots,) + field, f32),
                dma((5,)),
                dma((5,)),
                dma((2,)),
                dma((2,)),
                dma((slots,)),
                dma((slots,)),
                dma((slots,)),
                dma((slots,)),
            ],
            compiler_params=pltpu.CompilerParams(
                collective_id=0, has_side_effects=True, vmem_limit_bytes=32 << 20
            ),
        )(iterate, forcing, initial, *rest)

    placed = (
        P(("groups", "tm"), None, "space"),
        P(("groups", "tm"), None, "space"),
        P("groups", "space"),
        P(),
        P(),
        P("space"),
        P(None, "space"),
        P(None, "space"),
        P(("groups", "tm"), None, "space"),
    )
    return jax.shard_map(
        local,
        mesh=mesh,
        in_specs=placed,
        out_specs=P(("groups", "tm"), None, "space"),
        check_vma=False,
    )
```

```python
import functools

import jax
import jax.numpy as jnp
from jax import lax
from jax.experimental import pallas as pl
from jax.experimental.pallas import tpu as pltpu
from jax.sharding import PartitionSpec as P

CF = 4
BND = 64
LANES = 128
MESH = pl.DeviceIdType.MESH


def radices(count):
    out = []
    while count > 1:
        for m in (4, 2, count):
            if count % m == 0:
                out.append(m)
                count //= m
                break
    return out or [1]


def kernel(
    count,
    stages,
    iterate_at,
    forcing_at,
    initial_at,
    self_at,
    face_at,
    gain_at,
    neighbors_at,
    face_mask_at,
    decay_at,
    out,
    iterate,
    forcing,
    self_block,
    face_blocks,
    gain,
    neighbors,
    face_mask,
    decay,
    start,
    cur,
    source,
    partner_source,
    where_from,
    gains,
    weights,
    high,
    low,
    residual,
    entering,
    rslots,
    dslots,
    core_send,
    core_recv,
    step_send,
    step_recv,
    rsend,
    rrecv,
    dsend,
    drecv,
    loaded,
):
    f32, bf16 = jnp.float32, jnp.bfloat16
    g, t, s = (lax.axis_index(a) for a in ("groups", "tm", "space"))
    other = (g, t, 1 - s)
    rows, width = initial_at.shape

    loads = {}
    for i, (name, src, dst) in enumerate(
        (
            ("neighbors", neighbors_at, neighbors),
            ("face_mask", face_mask_at, face_mask),
            ("gain", gain_at, gain),
            ("decay", decay_at, decay),
            ("forcing", forcing_at, forcing),
            ("self_block", self_at, self_block),
            ("face_blocks", face_at, face_blocks),
            ("iterate", iterate_at, iterate),
            ("initial", initial_at, start.at[0]),
        )
    ):
        loads[name] = pltpu.make_async_copy(src, dst, loaded.at[i])
        if name != "initial":
            loads[name].start()

    @pl.when(t == 0)
    def _():
        loads["initial"].start()

    digits, strides, stride = [], [], 1
    for m in stages:
        digits.append(lax.rem(t // stride, m))
        strides.append(stride)
        stride *= m

    barrier = pltpu.get_barrier_semaphore()
    pl.semaphore_signal(barrier, inc=1, device_id=other, device_id_type=MESH)
    greeted = 1
    if count > 1:
        for by in (1, count - 1):
            for core in (s, 1 - s):
                there = (g, lax.rem(t + by, count), core)
                pl.semaphore_signal(barrier, inc=1, device_id=there, device_id_type=MESH)
                greeted += 1
        for m, digit, stride in zip(stages, digits, strides):
            for by in range(1, m):
                to = t + (lax.rem(digit + by, m) - digit) * stride
                pl.semaphore_signal(barrier, inc=1, device_id=(g, to, s), device_id_type=MESH)
                greeted += 1

    def to_core(src, dst, i):
        return pltpu.make_async_remote_copy(
            src, dst, core_send.at[i], core_recv.at[i], device_id=other, device_id_type=MESH
        )

    def shift(i):
        core = s if i == 0 else 1 - s
        to = lax.rem(t + 1, count)
        return pltpu.make_async_remote_copy(
            iterate_at.at[0],
            start.at[i],
            step_send.at[i],
            step_recv.at[i],
            device_id=(g, to, core),
            device_id_type=MESH,
        )

    first_half = to_core(initial_at, start.at[1], 0)
    table_copy = to_core(where_from.at[0], where_from.at[1], 1)
    gain_copy = to_core(gains.at[0], gains.at[1], 2)
    source_copy = to_core(source.at[pl.ds(0, CF - 1)], partner_source, 3)
    entering_copy = to_core(entering.at[0], entering.at[1], 4)

    pl.semaphore_wait(barrier, greeted)
    if count > 1:

        @pl.when(t < count - 1)
        def _():
            shift(0).start()
            shift(1).start()

    @pl.when(t == 0)
    def _():
        first_half.start()

    for name in ("neighbors", "face_mask", "gain"):
        loads[name].wait()
    where_from[0, 0:6, :] = jnp.where(face_mask[...] == 0, -1, neighbors[...])
    where_from[0, 6:8, :] = jnp.zeros((2, width), jnp.int32)
    gains[0] = jnp.broadcast_to(gain[...][None, :], (8, width))
    table_copy.start()
    gain_copy.start()

    def link(slots, send, recv, i, b):
        digit = digits[i]
        base = sum(stages[:i])
        return pltpu.make_async_remote_copy(
            slots.at[base + digit],
            slots.at[base + digit],
            send.at[base + b],
            recv.at[base + digit],
            device_id=(g, t + (b - digit) * strides[i], s),
            device_id_type=MESH,
        )

    def arrival(slots, send, recv, i, b):
        base = sum(stages[:i])
        return pltpu.make_async_remote_copy(
            slots.at[base + b],
            slots.at[base + b],
            send.at[base + b],
            recv.at[base + b],
            device_id=(g, t, s),
            device_id_type=MESH,
        )

    def each_out(i, act):
        for b in range(stages[i]):
            last = i == len(stages) - 1
            pl.when(b > digits[i] if last else b != digits[i])(functools.partial(act, b))

    def each_in(i, act):
        for b in range(stages[i]):
            last = i == len(stages) - 1
            pl.when(b < digits[i] if last else b != digits[i])(functools.partial(act, b))

    def send(slots, ss, rs, i, value):
        slots[sum(stages[:i]) + digits[i]] = value
        each_out(i, lambda b: link(slots, ss, rs, i, b).start())

    def receive(slots, ss, rs, i):
        each_in(i, lambda b: arrival(slots, ss, rs, i, b).wait_recv())

    loads["decay"].wait()
    damping = decay[0].astype(f32)
    send(dslots, dsend, drecv, 0, damping)
    loads["forcing"].wait()
    source[...] = forcing[...].astype(f32)
    source_copy.start()
    for name in ("self_block", "face_blocks", "iterate"):
        loads[name].wait()

    blocks = jnp.concatenate([self_block[...]] + [face_blocks[f] for f in range(6)], axis=1)
    upper = blocks.astype(bf16)
    weights[0:rows, :] = upper
    weights[rows : 2 * rows, :] = (blocks - upper.astype(f32)).astype(bf16)

    def put(r, cols, value):
        top = value.astype(bf16)
        high[r * rows : (r + 1) * rows, cols] = top
        low[r * rows : (r + 1) * rows, cols] = (value - top.astype(f32)).astype(bf16)

    def advance(field, halves):
        for h in range(halves):
            near = [field[h, :, LANES * i : LANES * (i + 1)] for i in range(width // LANES)]
            far = field[1 - h, :, width - LANES :]
            for i in range(width // LANES):
                cols = slice(h * width + LANES * i, h * width + LANES * (i + 1))
                put(0, cols, near[i])
                for f in range(6):
                    v = where_from[h, f : f + 1, LANES * i : LANES * (i + 1)]
                    lane = lax.bitwise_and(jnp.where(v >= width, v - BND, v), LANES - 1)
                    lane = jnp.broadcast_to(lane, (rows, LANES))
                    v = jnp.broadcast_to(v, (rows, LANES))
                    got = jnp.take_along_axis(far, lane, axis=1)
                    for k in reversed(range(width // LANES)):
                        here = jnp.take_along_axis(near[k], lane, axis=1)
                        got = jnp.where(v < LANES * (k + 1), here, got)
                    put(f + 1, cols, jnp.where(v < 0, 0.0, got))
        n = halves * width
        both = jnp.dot(weights[...], high[:, :n], preferred_element_type=f32)
        rest = jnp.dot(weights[0:rows, :], low[:, :n], preferred_element_type=f32)
        total = both[:rows] + (both[rows:] + rest)
        return [total[:, h * width : (h + 1) * width] * gains[h, 0:1, :] for h in range(halves)]

    if count > 1:

        @pl.when(t > 0)
        def _():
            shift(0).wait_recv()
            shift(1).wait_recv()

    @pl.when(t == 0)
    def _():
        loads["initial"].wait()
        first_half.wait_recv()

    table_copy.wait_recv()
    gain_copy.wait_recv()

    def decay_stage(i, product, before):
        receive(dslots, dsend, drecv, i)
        base = sum(stages[:i])
        lead = jnp.ones((rows, width), f32)
        whole = lead
        for b in range(stages[i]):
            part = dslots[base + b]
            lead = jnp.where(b < digits[i], lead * part, lead)
            whole = whole * part
        return whole, before * lead

    befores = [jnp.ones((rows, width), f32)]
    product = damping
    field = start
    for j in range(CF):
        got = advance(field, 2 if j < CF - 1 else 1)
        if j == 0:
            source_copy.wait_recv()
        if j < CF - 1:
            cur[0] = got[0] + source[j]
            cur[1] = got[1] + partner_source[j]
            field = cur
        if j == 1:
            for i in range(len(stages) - 1):
                product, after = decay_stage(i, product, befores[-1])
                befores.append(after)
                send(dslots, dsend, drecv, i + 1, product)
    local = (got[0] + source[CF - 1]) - iterate[0]
    residual[...] = local

    term = local
    prefix = jnp.zeros((rows, width), f32)
    for i in range(len(stages)):
        send(rslots, rsend, rrecv, i, term)
        base = sum(stages[:i])
        if i == len(stages) - 1:
            receive(dslots, dsend, drecv, i)
        receive(rslots, rsend, rrecv, i)
        carried = jnp.zeros((rows, width), f32)
        whole = carried
        for b in range(stages[i]):
            r, d = rslots[base + b], dslots[base + b]
            carried = jnp.where(b < digits[i], d * carried + r, carried)
            if i < len(stages) - 1:
                whole = d * whole + r
        prefix = prefix + befores[i] * carried
        term = whole
    entering[0] = prefix
    entering_copy.start()
    cur[0] = start[0] + prefix
    out[CF - 1] = iterate[0] + (damping * prefix + residual[...])
    entering_copy.wait_recv()
    cur[1] = start[1] + entering[1]
    for j in range(CF - 1):
        got = advance(cur, 2 if j < CF - 2 else 1)
        out[j] = got[0] + source[j]
        if j < CF - 2:
            cur[0] = out[j]
            cur[1] = got[1] + partner_source[j]

    for copy in (table_copy, gain_copy, source_copy, entering_copy):
        copy.wait_send()

    @pl.when(t == 0)
    def _():
        first_half.wait_send()

    if count > 1:

        @pl.when(t < count - 1)
        def _():
            shift(0).wait_send()
            shift(1).wait_send()

    for i in range(len(stages)):
        each_out(i, lambda b: link(dslots, dsend, drecv, i, b).wait_send())
        each_out(i, lambda b: link(rslots, rsend, rrecv, i, b).wait_send())


def solution(mesh):
    count = mesh.shape["tm"]
    stages = radices(count)
    slots = sum(stages)

    def local(iterate, forcing, initial, *rest):
        rows, width = initial.shape
        f32 = jnp.float32
        vmem = pl.BlockSpec(memory_space=pltpu.VMEM)
        hbm = pl.BlockSpec(memory_space=pltpu.HBM)
        operands = (iterate, forcing) + rest
        dma = pltpu.SemaphoreType.DMA
        field = (rows, width)
        return pl.pallas_call(
            functools.partial(kernel, count, stages),
            out_shape=jax.ShapeDtypeStruct((CF, rows, width), f32),
            in_specs=[hbm] * 9,
            out_specs=vmem,
            scratch_shapes=[pltpu.VMEM(a.shape, a.dtype) for a in operands]
            + [
                pltpu.VMEM((2,) + field, f32),
                pltpu.VMEM((2,) + field, f32),
                pltpu.VMEM((CF,) + field, f32),
                pltpu.VMEM((CF - 1,) + field, f32),
                pltpu.VMEM((2, 8, width), jnp.int32),
                pltpu.VMEM((2, 8, width), f32),
                pltpu.VMEM((2 * rows, 7 * rows), jnp.bfloat16),
                pltpu.VMEM((7 * rows, 2 * width), jnp.bfloat16),
                pltpu.VMEM((7 * rows, 2 * width), jnp.bfloat16),
                pltpu.VMEM(field, f32),
                pltpu.VMEM((2,) + field, f32),
                pltpu.VMEM((slots,) + field, f32),
                pltpu.VMEM((slots,) + field, f32),
                dma((5,)),
                dma((5,)),
                dma((2,)),
                dma((2,)),
                dma((slots,)),
                dma((slots,)),
                dma((slots,)),
                dma((slots,)),
                dma((9,)),
            ],
            compiler_params=pltpu.CompilerParams(
                collective_id=0, has_side_effects=True
            ),
        )(iterate, forcing, initial, *rest)

    placed = (
        P(("groups", "tm"), None, "space"),
        P(("groups", "tm"), None, "space"),
        P("groups", "space"),
        P(),
        P(),
        P("space"),
        P(None, "space"),
        P(None, "space"),
        P(("groups", "tm"), None, "space"),
    )
    return jax.shard_map(
        local,
        mesh=mesh,
        in_specs=placed,
        out_specs=P(("groups", "tm"), None, "space"),
        check_vma=False,
    )
```

```python
import functools

import jax
import jax.numpy as jnp
from jax import lax
from jax.experimental import pallas as pl
from jax.experimental.pallas import tpu as pltpu
from jax.sharding import PartitionSpec as P

CF = 4
BND = 64
LANES = 128
MESH = pl.DeviceIdType.MESH


def radices(count):
    out = []
    while count > 1:
        for m in (4, 2, count):
            if count % m == 0:
                out.append(m)
                count //= m
                break
    return out or [1]


def kernel(
    count,
    stages,
    iterate_at,
    forcing_at,
    initial_at,
    self_at,
    face_at,
    gain_at,
    neighbors_at,
    face_mask_at,
    decay_at,
    out_at,
    iterate,
    forcing,
    self_block,
    face_blocks,
    gain,
    neighbors,
    face_mask,
    decay,
    start,
    cur,
    source,
    partner_source,
    where_from,
    gains,
    weights,
    high,
    low,
    residual,
    entering,
    rslots,
    dslots,
    core_send,
    core_recv,
    step_send,
    step_recv,
    rsend,
    rrecv,
    dsend,
    drecv,
    loaded,
    out,
    stored,
):
    f32, bf16 = jnp.float32, jnp.bfloat16
    g, t, s = (lax.axis_index(a) for a in ("groups", "tm", "space"))
    other = (g, t, 1 - s)
    rows, width = initial_at.shape

    loads = {}
    for i, (name, src, dst) in enumerate(
        (
            ("neighbors", neighbors_at, neighbors),
            ("face_mask", face_mask_at, face_mask),
            ("gain", gain_at, gain),
            ("decay", decay_at, decay),
            ("forcing", forcing_at, forcing),
            ("self_block", self_at, self_block),
            ("face_blocks", face_at, face_blocks),
            ("iterate", iterate_at, iterate),
            ("initial", initial_at, start.at[0]),
        )
    ):
        loads[name] = pltpu.make_async_copy(src, dst, loaded.at[i])
        if name != "initial":
            loads[name].start()

    @pl.when(t == 0)
    def _():
        loads["initial"].start()

    digits, strides, stride = [], [], 1
    for m in stages:
        digits.append(lax.rem(t // stride, m))
        strides.append(stride)
        stride *= m

    barrier = pltpu.get_barrier_semaphore()
    pl.semaphore_signal(barrier, inc=1, device_id=other, device_id_type=MESH)
    greeted = 1
    if count > 1:
        for by in (1, count - 1):
            for core in (s, 1 - s):
                there = (g, lax.rem(t + by, count), core)
                pl.semaphore_signal(barrier, inc=1, device_id=there, device_id_type=MESH)
                greeted += 1
        for m, digit, stride in zip(stages, digits, strides):
            for by in range(1, m):
                to = t + (lax.rem(digit + by, m) - digit) * stride
                pl.semaphore_signal(barrier, inc=1, device_id=(g, to, s), device_id_type=MESH)
                greeted += 1

    def to_core(src, dst, i):
        return pltpu.make_async_remote_copy(
            src, dst, core_send.at[i], core_recv.at[i], device_id=other, device_id_type=MESH
        )

    def shift(i):
        core = s if i == 0 else 1 - s
        to = lax.rem(t + 1, count)
        return pltpu.make_async_remote_copy(
            iterate_at.at[0],
            start.at[i],
            step_send.at[i],
            step_recv.at[i],
            device_id=(g, to, core),
            device_id_type=MESH,
        )

    def store(j):
        return pltpu.make_async_copy(out.at[j], out_at.at[j], stored.at[j])

    first_half = to_core(initial_at, start.at[1], 0)
    table_copy = to_core(where_from.at[0], where_from.at[1], 1)
    gain_copy = to_core(gains.at[0], gains.at[1], 2)
    source_copy = to_core(source.at[pl.ds(0, CF - 1)], partner_source, 3)
    entering_copy = to_core(entering.at[0], entering.at[1], 4)

    pl.semaphore_wait(barrier, greeted)
    if count > 1:

        @pl.when(t < count - 1)
        def _():
            shift(0).start()
            shift(1).start()

    @pl.when(t == 0)
    def _():
        first_half.start()

    for name in ("neighbors", "face_mask", "gain"):
        loads[name].wait()
    where_from[0, 0:6, :] = jnp.where(face_mask[...] == 0, -1, neighbors[...])
    where_from[0, 6:8, :] = jnp.zeros((2, width), jnp.int32)
    gains[0] = jnp.broadcast_to(gain[...][None, :], (8, width))
    table_copy.start()
    gain_copy.start()

    def link(slots, send, recv, i, b):
        digit = digits[i]
        base = sum(stages[:i])
        return pltpu.make_async_remote_copy(
            slots.at[base + digit],
            slots.at[base + digit],
            send.at[base + b],
            recv.at[base + digit],
            device_id=(g, t + (b - digit) * strides[i], s),
            device_id_type=MESH,
        )

    def arrival(slots, send, recv, i, b):
        base = sum(stages[:i])
        return pltpu.make_async_remote_copy(
            slots.at[base + b],
            slots.at[base + b],
            send.at[base + b],
            recv.at[base + b],
            device_id=(g, t, s),
            device_id_type=MESH,
        )

    def each_out(i, act):
        for b in range(stages[i]):
            last = i == len(stages) - 1
            pl.when(b > digits[i] if last else b != digits[i])(functools.partial(act, b))

    def each_in(i, act):
        for b in range(stages[i]):
            last = i == len(stages) - 1
            pl.when(b < digits[i] if last else b != digits[i])(functools.partial(act, b))

    def send(slots, ss, rs, i, value):
        slots[sum(stages[:i]) + digits[i]] = value
        each_out(i, lambda b: link(slots, ss, rs, i, b).start())

    def receive(slots, ss, rs, i):
        each_in(i, lambda b: arrival(slots, ss, rs, i, b).wait_recv())

    loads["decay"].wait()
    damping = decay[0].astype(f32)
    send(dslots, dsend, drecv, 0, damping)
    loads["forcing"].wait()
    source[...] = forcing[...].astype(f32)
    source_copy.start()
    for name in ("self_block", "face_blocks", "iterate"):
        loads[name].wait()

    blocks = jnp.concatenate([self_block[...]] + [face_blocks[f] for f in range(6)], axis=1)
    upper = blocks.astype(bf16)
    weights[0:rows, :] = upper
    weights[rows : 2 * rows, :] = (blocks - upper.astype(f32)).astype(bf16)

    def put(r, cols, value):
        top = value.astype(bf16)
        high[r * rows : (r + 1) * rows, cols] = top
        low[r * rows : (r + 1) * rows, cols] = (value - top.astype(f32)).astype(bf16)

    def advance(field, halves):
        for h in range(halves):
            near = [field[h, :, LANES * i : LANES * (i + 1)] for i in range(width // LANES)]
            far = field[1 - h, :, width - LANES :]
            for i in range(width // LANES):
                cols = slice(h * width + LANES * i, h * width + LANES * (i + 1))
                put(0, cols, near[i])
                for f in range(6):
                    v = where_from[h, f : f + 1, LANES * i : LANES * (i + 1)]
                    lane = lax.bitwise_and(jnp.where(v >= width, v - BND, v), LANES - 1)
                    lane = jnp.broadcast_to(lane, (rows, LANES))
                    v = jnp.broadcast_to(v, (rows, LANES))
                    got = jnp.take_along_axis(far, lane, axis=1)
                    for k in reversed(range(width // LANES)):
                        here = jnp.take_along_axis(near[k], lane, axis=1)
                        got = jnp.where(v < LANES * (k + 1), here, got)
                    put(f + 1, cols, jnp.where(v < 0, 0.0, got))
        n = halves * width
        both = jnp.dot(weights[...], high[:, :n], preferred_element_type=f32)
        rest = jnp.dot(weights[0:rows, :], low[:, :n], preferred_element_type=f32)
        total = both[:rows] + (both[rows:] + rest)
        return [total[:, h * width : (h + 1) * width] * gains[h, 0:1, :] for h in range(halves)]

    if count > 1:

        @pl.when(t > 0)
        def _():
            shift(0).wait_recv()
            shift(1).wait_recv()

    @pl.when(t == 0)
    def _():
        loads["initial"].wait()
        first_half.wait_recv()

    table_copy.wait_recv()
    gain_copy.wait_recv()

    def decay_stage(i, product, before):
        receive(dslots, dsend, drecv, i)
        base = sum(stages[:i])
        lead = jnp.ones((rows, width), f32)
        whole = lead
        for b in range(stages[i]):
            part = dslots[base + b]
            lead = jnp.where(b < digits[i], lead * part, lead)
            whole = whole * part
        return whole, before * lead

    befores = [jnp.ones((rows, width), f32)]
    product = damping
    field = start
    for j in range(CF):
        got = advance(field, 2 if j < CF - 1 else 1)
        if j == 0:
            source_copy.wait_recv()
        if j < CF - 1:
            cur[0] = got[0] + source[j]
            cur[1] = got[1] + partner_source[j]
            field = cur
        if j == 1:
            for i in range(len(stages) - 1):
                product, after = decay_stage(i, product, befores[-1])
                befores.append(after)
                send(dslots, dsend, drecv, i + 1, product)
    local = (got[0] + source[CF - 1]) - iterate[0]
    residual[...] = local

    half = rows // 2
    parts = [slice(0, half), slice(half, rows)]

    def part_link(i, b, c, arriving):
        base = sum(stages[:i])
        own = b if arriving else digits[i]
        ref = rslots.at[base + own, parts[c]]
        to = t if arriving else t + (b - digits[i]) * strides[i]
        return pltpu.make_async_remote_copy(
            ref, ref, rsend.at[base + b, c], rrecv.at[base + own, c],
            device_id=(g, to, s), device_id_type=MESH,
        )

    def send_part(i, c, value):
        rslots[sum(stages[:i]) + digits[i], parts[c]] = value
        each_out(i, lambda b: part_link(i, b, c, False).start())

    for c in range(2):
        send_part(0, c, local[parts[c]])
    prefixes = [jnp.zeros((half, width), f32)] * 2
    for i in range(len(stages)):
        base = sum(stages[:i])
        if i == len(stages) - 1:
            receive(dslots, dsend, drecv, i)
        for c in range(2):
            each_in(i, lambda b: part_link(i, b, c, True).wait_recv())
            carried = jnp.zeros((half, width), f32)
            whole = carried
            for b in range(stages[i]):
                r, d = rslots[base + b, parts[c]], dslots[base + b, parts[c]]
                carried = jnp.where(b < digits[i], d * carried + r, carried)
                if i < len(stages) - 1:
                    whole = d * whole + r
            if i < len(stages) - 1:
                send_part(i + 1, c, whole)
            prefixes[c] = prefixes[c] + befores[i][parts[c]] * carried
    prefix = jnp.concatenate(prefixes, axis=0)
    entering[0] = prefix
    entering_copy.start()
    cur[0] = start[0] + prefix
    out[CF - 1] = iterate[0] + (damping * prefix + residual[...])
    store(CF - 1).start()
    entering_copy.wait_recv()
    cur[1] = start[1] + entering[1]
    for j in range(CF - 1):
        got = advance(cur, 2 if j < CF - 2 else 1)
        out[j] = got[0] + source[j]
        store(j).start()
        if j < CF - 2:
            cur[0] = out[j]
            cur[1] = got[1] + partner_source[j]

    for j in range(CF):
        store(j).wait()
    for copy in (table_copy, gain_copy, source_copy, entering_copy):
        copy.wait_send()

    @pl.when(t == 0)
    def _():
        first_half.wait_send()

    if count > 1:

        @pl.when(t < count - 1)
        def _():
            shift(0).wait_send()
            shift(1).wait_send()

    for i in range(len(stages)):
        each_out(i, lambda b: link(dslots, dsend, drecv, i, b).wait_send())
        for c in range(2):
            each_out(i, lambda b: part_link(i, b, c, False).wait_send())


def solution(mesh):
    count = mesh.shape["tm"]
    stages = radices(count)
    slots = sum(stages)

    def local(iterate, forcing, initial, *rest):
        rows, width = initial.shape
        f32 = jnp.float32
        hbm = pl.BlockSpec(memory_space=pltpu.HBM)
        operands = (iterate, forcing) + rest
        dma = pltpu.SemaphoreType.DMA
        field = (rows, width)
        return pl.pallas_call(
            functools.partial(kernel, count, stages),
            out_shape=jax.ShapeDtypeStruct((CF, rows, width), f32),
            in_specs=[hbm] * 9,
            out_specs=hbm,
            scratch_shapes=[pltpu.VMEM(a.shape, a.dtype) for a in operands]
            + [
                pltpu.VMEM((2,) + field, f32),
                pltpu.VMEM((2,) + field, f32),
                pltpu.VMEM((CF,) + field, f32),
                pltpu.VMEM((CF - 1,) + field, f32),
                pltpu.VMEM((2, 8, width), jnp.int32),
                pltpu.VMEM((2, 8, width), f32),
                pltpu.VMEM((2 * rows, 7 * rows), jnp.bfloat16),
                pltpu.VMEM((7 * rows, 2 * width), jnp.bfloat16),
                pltpu.VMEM((7 * rows, 2 * width), jnp.bfloat16),
                pltpu.VMEM(field, f32),
                pltpu.VMEM((2,) + field, f32),
                pltpu.VMEM((slots,) + field, f32),
                pltpu.VMEM((slots,) + field, f32),
                dma((5,)),
                dma((5,)),
                dma((2,)),
                dma((2,)),
                dma((slots, 2)),
                dma((slots, 2)),
                dma((slots,)),
                dma((slots,)),
                dma((9,)),
                pltpu.VMEM((CF,) + field, f32),
                dma((CF,)),
            ],
            compiler_params=pltpu.CompilerParams(
                collective_id=0, has_side_effects=True
            ),
        )(iterate, forcing, initial, *rest)

    placed = (
        P(("groups", "tm"), None, "space"),
        P(("groups", "tm"), None, "space"),
        P("groups", "space"),
        P(),
        P(),
        P("space"),
        P(None, "space"),
        P(None, "space"),
        P(("groups", "tm"), None, "space"),
    )
    return jax.shard_map(
        local,
        mesh=mesh,
        in_specs=placed,
        out_specs=P(("groups", "tm"), None, "space"),
        check_vma=False,
    )
```
